256 devices in a mesh: dir: 64 (over x, z, core), box: 4 (over y).
Axes of the slice: x: 4, y: 4, z: 8, core: 2. Of those that a mesh axis runs over, the one named last changes fastest.
Arguments:
- wedge_local: bfloat16 [4096, 64, 256], P('box', 'dir'), may hold values from -6 to 6
- wedge_ops: bfloat16 [16384, 512], P(('dir', 'box')), may hold values from -0.046875 to 0.046875
- octant_angle: float32 [8, 64, 128], replicated, may hold values from -3.140625 to 3.140625
- child_box: int32 [49152], P(('box', 'dir')), may hold values from -1 to 32767, as said below
Outputs:
- child_local: bfloat16 [49152, 512], P(('box', 'dir'))
The draws below stay inside these ranges and needn't reach their ends.
Inputs may be any that keep to these rules, and one draw needn't show every extreme that they name: `child_box`: taking the slots in blocks of 192 (block j = b * 64 + d for box range b), block j holds consecutive Morton child indices from its first slot on and -1 after them; the blocks of box range b together hold every child of parents b * 16 * 64 to (b + 1) * 16 * 64 - 1 once, in order, and the children of block j have parents within 4 boxes of parents (b * 64 + d) * 16 to (b * 64 + d + 1) * 16 - 1. Every draw fills some block completely.
All inputs are finite; a program needn't handle non-finite values.
Results may differ from the reference program's by a relative error of at most 0.0049.
Values may be sent and summed in bfloat16 or wider, within the bound.
A program may use at most 128 MiB of HBM per device.

```python
import math
import jax
import jax.numpy as jnp
from jax import lax

WEDGES = 64
COEF = 256
QCOEF = 512
PAR_DEV = 16
HALO = 4
SLOT_DEV = 192
PARENTS = 4096
N_DIR = 64
N_BOX = 4


def draw_child_box(key, part):
    key = jax.random.fold_in(key, 7)
    first_key, second_key = jax.random.split(key)
    offsets = jax.random.randint(first_key, (N_BOX, N_DIR + 1), -8 * HALO, 8 * HALO + 1)
    picked = jax.random.randint(second_key, (N_BOX, 1), 1, N_DIR - 1)
    bounds_index = jnp.arange(N_DIR + 1, dtype=jnp.int32)[None, :]
    offsets = jnp.where(bounds_index == picked, -8 * HALO, offsets)
    offsets = jnp.where(bounds_index == picked + 1, 8 * HALO, offsets)
    offsets = jnp.where((bounds_index == 0) | (bounds_index == N_DIR), 0, offsets)
    bounds = 8 * PAR_DEV * bounds_index + offsets
    starts = bounds[:, :-1]
    counts = bounds[:, 1:] - starts
    slot_index = jnp.arange(SLOT_DEV, dtype=jnp.int32)[None, None, :]
    base = jnp.arange(N_BOX, dtype=jnp.int32)[:, None, None] * (8 * PAR_DEV * N_DIR)
    values = base + starts[:, :, None] + slot_index
    values = jnp.where(slot_index < counts[:, :, None], values, -1)
    return values.reshape(-1).astype(jnp.int32)


def block_levels(own_key, shape, cuts, smallest, top_value):
    level, own = 1.0, jax.random.fold_in(own_key, 6)
    for position, parts in cuts:
        draws = jnp.exp(jax.random.uniform(jax.random.fold_in(own, position), (parts,), jnp.float32, smallest / len(cuts), top_value / len(cuts)))
        level = level * jnp.repeat(draws, shape[position] // parts).reshape([-1 if axis == position else 1 for axis in range(len(shape))])
    return level


def bell_draw(own_key, shape, scale, limit, pieces=(), kind=jnp.bfloat16):
    level = block_levels(own_key, shape, pieces, -0.22, 0.18) if pieces else 1.0
    result = jax.random.normal(own_key, shape, jnp.float32) * scale * level
    return jnp.minimum(jnp.maximum(result, -limit), limit).astype(kind)


def setup_inputs(seed: int = 0) -> dict:
    key_of = jax.random.split(jax.random.key(seed), 5)
    wedge_local = bell_draw(key_of[0], (PARENTS, WEDGES, COEF), 1.0, 6.0, ((0, 4), (1, 64)))
    wedge_ops = bell_draw(key_of[1], (WEDGES * COEF, QCOEF), (WEDGES * COEF) ** -0.5, 0.046875, ((0, 256),))
    octant_angle = jnp.clip(jax.random.uniform(key_of[2], (8, WEDGES, COEF // 2), jnp.float32, -3.140625, 3.140625), -3.140625, 3.140625)
    child_box = draw_child_box(jax.random.fold_in(key_of[4], 71), 0)
    return {"wedge_local": wedge_local, "wedge_ops": wedge_ops, "octant_angle": octant_angle, "child_box": child_box}


def rotate(values, angles):
    halves = values.shape[-1] // 2
    real_part = values[..., :halves]
    imag_part = values[..., halves:]
    cosine = jnp.cos(angles)
    sine_vals = jnp.sin(angles)
    return jnp.concatenate([real_part * cosine - imag_part * sine_vals, real_part * sine_vals + imag_part * cosine], axis=-1)


def reference(wedge_local, wedge_ops, octant_angle, child_box):
    parents = wedge_local.shape[0]
    wedges = wedge_local.shape[1]
    width = wedge_local.shape[2]
    step_rows = math.gcd(parents, 64)
    operator = wedge_ops.astype(jnp.float32)

    def one_block(parent_rows):
        shifted = rotate(parent_rows.astype(jnp.float32)[:, None], octant_angle[None]).astype(jnp.bfloat16)
        shifted = lax.optimization_barrier(shifted).astype(jnp.float32)
        flat_rows = shifted.reshape(-1, wedges * width)
        return jnp.dot(flat_rows, operator, precision=lax.Precision.HIGHEST).astype(jnp.bfloat16)

    stacked = wedge_local.reshape(parents // step_rows, step_rows, wedges, width)
    children = lax.map(one_block, stacked).reshape(parents * 8, wedge_ops.shape[1])
    occupied = child_box >= 0
    chosen = jnp.where(occupied, child_box, 0).astype(jnp.int32)
    return jnp.where(occupied[:, None], children[chosen], jnp.zeros((), jnp.bfloat16)).astype(jnp.bfloat16)
```

```python
import functools

import jax
import jax.numpy as jnp
from jax import lax
from jax.experimental import pallas as pl
from jax.experimental.pallas import tpu as pltpu
from jax.sharding import PartitionSpec as P

MESH = pl.DeviceIdType.MESH
NX, NZ, NC, NY = 4, 8, 2, 4
PAR = 16
HALO = 4
WIN = PAR + 2 * HALO
Q = 2


def kernel(ang_ref, a_ref, b_ref, out_ref, cs_ref, sn_ref, e_ref, abuf, op, bbuf, own, cpart, crecv, win,
           la_sem, lb_sem, as_sem, ar_sem, xs_sem, xr_sem, ys_sem, yr_sem, fs_sem, fr_sem,
           cs_sem, cr_sem, hs_sem, hr_sem):
    d = lax.axis_index("dir")
    y = lax.axis_index("box")
    c = d % NC
    z = (d // NC) % NZ
    x = d // (NC * NZ)
    cols = op.shape[1] // (NX * NC)
    wide = bbuf.shape[-1]
    half = cols // 2
    rows = PAR * 8

    def dev(dx=0, dy=0, dz=0, dc=0):
        return ((((x + dx) % NX) * NZ + (z + dz) % NZ) * NC + (c + dc) % NC, (y + dy) % NY)

    lower = ((d + NX * NZ * NC - 1) % (NX * NZ * NC), y)
    upper = ((d + 1) % (NX * NZ * NC), y)
    corner = ((d + NX * NZ * NC - 1 + 2 * c) % (NX * NZ * NC), y)
    sibling = dev(dc=1)

    barrier = pltpu.get_barrier_semaphore()
    peers = [dev(dx=i, dc=j) for i in range(NX) for j in range(NC) if i or j]
    peers += [dev(dy=i) for i in range(1, NY)]
    peers += [dev(dz=i) for i in range(1, NZ)]
    peers += [corner]
    for p in peers:
        pl.semaphore_signal(barrier, inc=1, device_id=p, device_id_type=MESH)

    def remote(src, dst, send, recv, to):
        return pltpu.make_async_remote_copy(
            src_ref=src, dst_ref=dst, send_sem=send, recv_sem=recv, device_id=to, device_id_type=MESH)

    sent = []

    def push(*args):
        copy = remote(*args)
        copy.start()
        sent.append(copy)

    def arrived(ref, sem):
        remote(ref, ref, sem, sem, sibling).wait_recv()

    me = x * NC + c
    own_a = pltpu.make_async_copy(a_ref.at[x, :, c], abuf.at[me], la_sem)
    own_a.start()
    own_b = [pltpu.make_async_copy(b_ref.at[:, pl.ds(q * wide, wide)], bbuf.at[q, x, c, y], lb_sem.at[q])
             for q in range(Q)]
    for copy in own_b:
        copy.start()

    e_ref[...] = (lax.broadcasted_iota(jnp.int32, e_ref.shape, 0) // 8
                  == lax.broadcasted_iota(jnp.int32, e_ref.shape, 1)).astype(e_ref.dtype)
    for i in range(NX):
        for j in range(NC):
            angle = ang_ref[:, pl.ds(i * NZ * NC + z * NC + j, 1), :].reshape(8, half)
            cs_ref[i * NC + j] = jnp.cos(angle)
            sn_ref[i * NC + j] = jnp.sin(angle)

    pl.semaphore_wait(barrier, len(peers))

    def send_own(q):
        block = b_ref.at[:, pl.ds(q * wide, wide)]
        for i in (1, 3, 2):
            push(block, bbuf.at[q, x, c, y], xs_sem.at[q, i], xr_sem.at[q, i], dev(dx=i))
        for i in (1, 3, 2):
            push(block, bbuf.at[q, x, c, y], ys_sem.at[q, 0, i], yr_sem.at[q, 0, i], dev(dy=i))

    send_own(0)
    for i in (2, 1, 3, 0):
        for j in range(NC):
            if i or j:
                push(a_ref.at[(x + i) % NX, :, (c + j) % NC], abuf.at[me],
                     as_sem.at[i * NC + j], ar_sem.at[i * NC + j], dev(dx=i, dc=j))
    send_own(1)

    def spread(q):
        for i in (1, 3, 2):
            slot = bbuf.at[q, (x + NX - i) % NX, c, y]
            arrived(slot, xr_sem.at[q, i])
            for k in (1, 3, 2):
                push(slot, slot, ys_sem.at[q, i, k], yr_sem.at[q, i, k], dev(dy=k))
        own_b[q].wait()
        group = bbuf.at[q, :, c, y]
        push(group, group, fs_sem.at[q, 0], fr_sem.at[q, 0], sibling)

    def collect(q):
        for k in (1, 3, 2):
            group = bbuf.at[q, :, c, (y + NY - k) % NY]
            for i in range(NX):
                arrived(bbuf.at[q, (x + NX - i) % NX, c, (y + NY - k) % NY], yr_sem.at[q, i, k])
            push(group, group, fs_sem.at[q, k], fr_sem.at[q, k], sibling)
        for k in range(NY):
            arrived(bbuf.at[q, :, (c + 1) % NC, (y + NY - k) % NY], fr_sem.at[q, k])

    def turn(k):
        wedge = abuf[k].reshape(rows, cols)
        values = jnp.dot(e_ref[...], wedge, preferred_element_type=jnp.float32).reshape(rows, 8, cols)
        re, im = values[..., :half], values[..., half:]
        cosine, sine = cs_ref[k][None], sn_ref[k][None]
        place = pl.multiple_of(k * cols, cols)
        op[:, pl.ds(place, half)] = (re * cosine - im * sine).astype(op.dtype).reshape(rows * 8, half)
        op[:, pl.ds(place + half, half)] = (re * sine + im * cosine).astype(op.dtype).reshape(rows * 8, half)

    spread(0)
    own_a.wait()
    turn(me)
    for i in (0, 1, 3, 2):
        for j in range(NC):
            if i or j:
                k = ((x + NX - i) % NX) * NC + (c + j) % NC
                arrived(abuf.at[k], ar_sem.at[i * NC + j])
                turn(k)
    spread(1)

    def multiply(q):
        weights = bbuf[q].reshape(op.shape[1], wide)
        for i in (2, 1, 3, 0):
            pair = (z // 2 + i) % (NZ // 2)
            lines = op[pl.ds(pl.multiple_of(pair * 2 * rows, 2 * rows), 2 * rows), :]
            part = jnp.dot(lines, weights, preferred_element_type=jnp.float32)
            if i == 0:
                own[q] = part.reshape(2, rows, wide)
            cpart[q, pair] = part.astype(cpart.dtype).reshape(2, rows, wide)
            for k in range(2):
                if i:
                    to = pair * 2 + k
                    push(cpart.at[q, pair, k], crecv.at[q, z], cs_sem.at[q, i, k], cr_sem.at[q, z],
                         ((x * NZ + to) * NC + c, y))
                elif k:
                    to = z + 1 - 2 * (z % 2)
                    push(cpart.at[q, pair, to % 2], crecv.at[q, z], cs_sem.at[q, 0, 1], cr_sem.at[q, z],
                         ((x * NZ + to) * NC + c, y))

    def total(q):
        value = own[q, z % 2]
        for i in (1, 7, 2, 6, 3, 5, 4):
            src = (z + i) % NZ
            arrived(crecv.at[q, src], cr_sem.at[q, src])
            value = value + crecv[q, src].astype(jnp.float32)
        here = pl.ds(q * wide, wide)
        edge = HALO * 8
        win[pl.ds(edge, rows), here] = value.astype(win.dtype)
        push(win.at[pl.ds(edge, edge), here], win.at[pl.ds(edge + rows, edge), here],
             hs_sem.at[q, 0], hr_sem.at[q, 0], lower)
        push(win.at[pl.ds(rows, edge), here], win.at[pl.ds(0, edge), here],
             hs_sem.at[q, 1], hr_sem.at[q, 1], upper)

    for q in range(Q):
        collect(q)
        multiply(q)
    for q in range(Q):
        total(q)
    edge = HALO * 8
    for q in range(Q):
        here = pl.ds(q * wide, wide)
        arrived(win.at[pl.ds(edge + rows, edge), here], hr_sem.at[q, 0])
        arrived(win.at[pl.ds(0, edge), here], hr_sem.at[q, 1])
    out_ref[...] = win[...]
    for copy in sent:
        copy.wait_send()


def exchange(angle, a, b):
    cols, wide = a.shape[-1], b.shape[1] // Q
    rows = PAR * 8
    depth = NX * NC * cols
    dma = pltpu.SemaphoreType.DMA
    bf16, f32 = jnp.bfloat16, jnp.float32
    return pl.pallas_call(
        kernel,
        out_shape=jax.ShapeDtypeStruct((WIN * 8, b.shape[1]), bf16),
        in_specs=[pl.BlockSpec(memory_space=pltpu.VMEM), pl.BlockSpec(memory_space=pl.ANY),
                  pl.BlockSpec(memory_space=pl.ANY)],
        out_specs=pl.BlockSpec(memory_space=pltpu.VMEM),
        scratch_shapes=[
            pltpu.VMEM((NX * NC, 8, cols // 2), f32),
            pltpu.VMEM((NX * NC, 8, cols // 2), f32),
            pltpu.VMEM((rows * 8, rows), bf16),
            pltpu.VMEM((NX * NC, NZ, PAR, cols), bf16),
            pltpu.VMEM((rows * 8, depth), bf16),
            pltpu.VMEM((Q, NX, NC, NY, cols // NY, wide), bf16),
            pltpu.VMEM((Q, 2, rows, wide), f32),
            pltpu.VMEM((Q, NZ // 2, 2, rows, wide), bf16),
            pltpu.VMEM((Q, NZ, rows, wide), bf16),
            pltpu.VMEM((WIN * 8, b.shape[1]), bf16),
            dma, dma((Q,)),
            dma((NX * NC,)), dma((NX * NC,)),
            dma((Q, NX)), dma((Q, NX)),
            dma((Q, NX, NY)), dma((Q, NX, NY)),
            dma((Q, NY)), dma((Q, NY)),
            dma((Q, NZ // 2, 2)), dma((Q, NZ)),
            dma((Q, 2)), dma((Q, 2)),
        ],
        compiler_params=pltpu.CompilerParams(
            collective_id=0, has_side_effects=True, vmem_limit_bytes=40 * 1024 * 1024),
    )(angle, a, b)


def on_device(wedge_local, wedge_ops, octant_angle, child_box):
    a = wedge_local.reshape(NX, NZ, NC, PAR, wedge_local.shape[-1])
    window = exchange(octant_angle, a, wedge_ops)
    block = lax.axis_index("box") * (NX * NZ * NC) + lax.axis_index("dir")
    first = (block * PAR - HALO) * 8
    place = jnp.where(child_box >= 0, child_box - first, -1)
    pick = (place[:, None] == jnp.arange(WIN * 8, dtype=jnp.int32)[None, :]).astype(jnp.bfloat16)
    return jnp.dot(pick, window, preferred_element_type=jnp.float32).astype(jnp.bfloat16)


def solution(mesh):
    placed = (P("box", "dir", None), P(("dir", "box"), None), P(), P(("box", "dir")))
    return jax.shard_map(
        on_device, mesh=mesh, in_specs=placed, out_specs=P(("box", "dir"), None), check_vma=False
    )
```

```python
import functools

import jax
import jax.numpy as jnp
from jax import lax
from jax.experimental import pallas as pl
from jax.experimental.pallas import tpu as pltpu
from jax.sharding import PartitionSpec as P

MESH = pl.DeviceIdType.MESH
NX, NZ, NC, NY = 4, 8, 2, 4
PAR = 16
HALO = 4
WIN = PAR + 2 * HALO
Q = 2
R = 2


def kernel(ang_hbm, a_ref, b_ref, box_hbm, out_ref, box_ref, ang_ref, cs_ref, sn_ref, e_ref, abuf, op, bbuf, acc, cpart, relay, near, far, mid,
           relayed, win, lc_sem, lg_sem, la_sem, lb_sem, as_sem, ar_sem, xs_sem, xr_sem, ys_sem, yr_sem, fs_sem, fr_sem,
           cs_sem, cr_sem, hs_sem, hr_sem):
    d = lax.axis_index("dir")
    y = lax.axis_index("box")
    c = d % NC
    z = (d // NC) % NZ
    x = d // (NC * NZ)
    cols = op.shape[1] // (NX * NC)
    wide = bbuf.shape[-1]
    half = cols // 2
    edge = HALO * 8
    part = PAR * 8 // R

    def dev(dx=0, dy=0, dz=0, dc=0):
        return ((((x + dx) % NX) * NZ + (z + dz) % NZ) * NC + (c + dc) % NC, (y + dy) % NY)

    lower = ((d + NX * NZ * NC - 1) % (NX * NZ * NC), y)
    upper = ((d + 1) % (NX * NZ * NC), y)
    corner = ((d + NX * NZ * NC - 1 + 2 * c) % (NX * NZ * NC), y)
    sibling = dev(dc=1)

    barrier = pltpu.get_barrier_semaphore()
    peers = [dev(dx=i, dc=j) for i in range(NX) for j in range(NC) if i or j]
    peers += [dev(dy=i) for i in range(1, NY)]
    peers += [dev(dz=i) for i in (1, 2, NZ - 2, NZ - 1)]
    peers += [corner]
    for p in peers:
        pl.semaphore_signal(barrier, inc=1, device_id=p, device_id_type=MESH)

    def remote(src, dst, send, recv, to):
        return pltpu.make_async_remote_copy(
            src_ref=src, dst_ref=dst, send_sem=send, recv_sem=recv, device_id=to, device_id_type=MESH)

    sent = []

    def push(*args):
        copy = remote(*args)
        copy.start()
        sent.append(copy)

    def arrived(ref, sem):
        remote(ref, ref, sem, sem, sibling).wait_recv()

    angles = pltpu.make_async_copy(ang_hbm, ang_ref, lg_sem)
    angles.start()
    boxes = pltpu.make_async_copy(box_hbm, box_ref, lc_sem)
    boxes.start()
    me = x * NC + c
    own_a = pltpu.make_async_copy(a_ref.at[x, :, c], abuf.at[me], la_sem)
    own_a.start()
    own_b = [pltpu.make_async_copy(b_ref.at[:, pl.ds(q * wide, wide)], bbuf.at[q, x, c, y], lb_sem.at[q])
             for q in range(Q)]
    for copy in own_b:
        copy.start()

    pl.semaphore_wait(barrier, len(peers))

    def send_own(q):
        block = b_ref.at[:, pl.ds(q * wide, wide)]
        for i in (2, 1, 3):
            push(block, bbuf.at[q, x, c, y], xs_sem.at[q, i], xr_sem.at[q, i], dev(dx=i))
        for i in (2, 1, 3):
            push(block, bbuf.at[q, x, c, y], ys_sem.at[q, 0, i], yr_sem.at[q, 0, i], dev(dy=i))

    for q in range(Q):
        send_own(q)
    for i in (2, 1, 3, 0):
        for j in range(NC):
            if i or j:
                push(a_ref.at[(x + i) % NX, :, (c + j) % NC], abuf.at[me],
                     as_sem.at[i * NC + j], ar_sem.at[i * NC + j], dev(dx=i, dc=j))

    row = lax.broadcasted_iota(jnp.int32, e_ref.shape, 0)
    place = (row // 8) % (PAR // R)
    place = jnp.where(row < NZ * part, jnp.where(place < HALO, place, place + PAR - 2 * HALO), place + HALO)
    e_ref[...] = ((row // part) % NZ * PAR + place
                  == lax.broadcasted_iota(jnp.int32, e_ref.shape, 1)).astype(e_ref.dtype)
    angles.wait()
    for i in range(NX):
        for j in range(NC):
            angle = ang_ref[:, pl.ds(i * NZ * NC + z * NC + j, 1), :].reshape(8, half)
            cs_ref[i * NC + j] = jnp.cos(angle)
            sn_ref[i * NC + j] = jnp.sin(angle)

    boxes.wait()
    first = ((y * (NX * NZ * NC) + d) * PAR - HALO) * 8
    place = box_ref[...] - first
    place = jnp.where(place < 2 * edge, place, jnp.where(
        place < 4 * edge, place + edge, jnp.where(place < 5 * edge, place - 2 * edge, place)))
    place = jnp.where(box_ref[...] >= 0, place, -1)
    pick = (lax.broadcasted_iota(jnp.int32, (WIN * 8, place.shape[1]), 0) == place).astype(win.dtype)

    def spread(q):
        for i in (1, 3, 2):
            slot = bbuf.at[q, (x + NX - i) % NX, c, y]
            arrived(slot, xr_sem.at[q, i])
            for k in (1, 3, 2):
                push(slot, slot, ys_sem.at[q, i, k], yr_sem.at[q, i, k], dev(dy=k))

    def collect(q, i):
        if i == 0:
            own_b[q].wait()
        for k in (1, 3, 2):
            arrived(bbuf.at[q, (x + NX - i) % NX, c, (y + NY - k) % NY], yr_sem.at[q, i, k])
        group = bbuf.at[q, (x + NX - i) % NX, c]
        push(group, group, fs_sem.at[q, i], fr_sem.at[q, i], sibling)

    def complete(q):
        for i in range(NX):
            arrived(bbuf.at[q, (x + NX - i) % NX, (c + 1) % NC], fr_sem.at[q, i])

    def turn(k, r):
        rows = NZ * part
        wedge = abuf[k].reshape(NZ * PAR, cols)
        chosen = e_ref[pl.ds(r * rows, rows), :]
        values = jnp.dot(chosen, wedge, preferred_element_type=jnp.float32).reshape(rows // 8, 8, cols)
        re, im = values[..., :half], values[..., half:]
        cosine, sine = cs_ref[k][None], sn_ref[k][None]
        column = pl.multiple_of(k * cols, cols)
        lines = pl.ds(r * rows, rows)
        op[lines, pl.ds(column, half)] = (re * cosine - im * sine).astype(op.dtype).reshape(rows, half)
        op[lines, pl.ds(column + half, half)] = (re * sine + im * cosine).astype(op.dtype).reshape(rows, half)

    for q in range(Q):
        spread(q)
    for q in range(Q):
        collect(q, 0)
    collect(0, 1)
    own_a.wait()
    turn(me, 0)
    for i in (0, 1, 3, 2):
        for j in range(NC):
            if i or j:
                k = ((x + NX - i) % NX) * NC + (c + j) % NC
                arrived(abuf.at[k], ar_sem.at[i * NC + j])
                turn(k, 0)

    narrow = wide // 2

    def multiply(q, r):
        lines = op[pl.ds(r * NZ * part, NZ * part), :]
        weights = bbuf[q].reshape(op.shape[1], wide)
        sums = jnp.dot(lines, weights, preferred_element_type=jnp.float32)
        acc[q, r] = sums.reshape(NZ, part, wide)
        cpart[q, r] = sums.astype(cpart.dtype).reshape(NZ, part, wide)
        for s, sign in enumerate((1, -1)):
            push(cpart.at[q, r, (z + NZ + 3 * sign) % NZ], mid.at[q, r, s],
                 cs_sem.at[q, r, 2 + s], cr_sem.at[q, r, 2 + s], dev(dz=NZ + sign))
        for s, sign in enumerate((1, -1)):
            push(cpart.at[q, r, (z + NZ // 2) % NZ, :, pl.ds(s * narrow, narrow)], far.at[q, r, s],
                 cs_sem.at[q, r, 4 + s], cr_sem.at[q, r, 4 + s], dev(dz=NZ + 2 * sign))

    def adjacent(q, r):
        for s, sign in enumerate((1, -1)):
            push(cpart.at[q, r, (z + NZ + sign) % NZ], near.at[q, r, s],
                 cs_sem.at[q, r, s], cr_sem.at[q, r, s], dev(dz=NZ + sign))

    def forward(q, r):
        for s, sign in enumerate((1, -1)):
            arrived(mid.at[q, r, s], cr_sem.at[q, r, 2 + s])
            arrived(far.at[q, r, s], cr_sem.at[q, r, 4 + s])
            value = acc[q, r, (z + NZ + 2 * sign) % NZ] + mid[q, r, s].astype(jnp.float32)
            extra = far[q, r, s].astype(jnp.float32)
            here, other = pl.ds(s * narrow, narrow), pl.ds((1 - s) * narrow, narrow)
            relay[q, r, s, :, here] = (value[:, s * narrow:(s + 1) * narrow] + extra).astype(relay.dtype)
            relay[q, r, s, :, other] = value[:, (1 - s) * narrow:(2 - s) * narrow].astype(relay.dtype)
            push(relay.at[q, r, s], relayed.at[q, r, s],
                 cs_sem.at[q, r, 6 + s], cr_sem.at[q, r, 6 + s], dev(dz=NZ + 2 * sign))

    def total(q, r):
        value = acc[q, r, z]
        for s in range(2):
            arrived(near.at[q, r, s], cr_sem.at[q, r, s])
            value = value + near[q, r, s].astype(jnp.float32)
        for s in range(2):
            arrived(relayed.at[q, r, s], cr_sem.at[q, r, 6 + s])
            value = value + relayed[q, r, s].astype(jnp.float32)
        here = pl.ds(q * wide, wide)
        win[pl.ds(edge + r * part, part), here] = value.astype(win.dtype)
        if r == 0:
            push(win.at[pl.ds(edge, edge), here], win.at[pl.ds(5 * edge, edge), here],
                 hs_sem.at[q, 0], hr_sem.at[q, 0], lower)
            push(win.at[pl.ds(2 * edge, edge), here], win.at[pl.ds(0, edge), here],
                 hs_sem.at[q, 1], hr_sem.at[q, 1], upper)

    collect(0, 3)
    collect(0, 2)
    complete(0)
    multiply(0, 0)
    for k in range(NX * NC):
        turn(k, 1)
    multiply(0, 1)
    adjacent(0, 0)
    for i in (1, 3, 2):
        collect(1, i)
    complete(1)
    multiply(1, 0)
    multiply(1, 1)
    for r in range(R):
        for q in range(Q):
            if q or r:
                adjacent(q, r)
    for r in range(R):
        for q in range(Q):
            forward(q, r)
    for r in range(R):
        for q in range(Q):
            total(q, r)
    for q in range(Q):
        here = pl.ds(q * wide, wide)
        arrived(win.at[pl.ds(5 * edge, edge), here], hr_sem.at[q, 0])
        arrived(win.at[pl.ds(0, edge), here], hr_sem.at[q, 1])
    out_ref[...] = lax.dot_general(
        pick, win[...], (((0,), (0,)), ((), ())), preferred_element_type=jnp.float32).astype(out_ref.dtype)
    for copy in sent:
        copy.wait_send()


def exchange(angle, a, b, boxes):
    cols, wide = a.shape[-1], b.shape[1] // Q
    rows = PAR * 8
    part = rows // R
    depth = NX * NC * cols
    dma = pltpu.SemaphoreType.DMA
    bf16, f32 = jnp.bfloat16, jnp.float32
    return pl.pallas_call(
        kernel,
        out_shape=jax.ShapeDtypeStruct((boxes.shape[1], b.shape[1]), bf16),
        in_specs=[pl.BlockSpec(memory_space=pltpu.HBM)] * 4,
        out_specs=pl.BlockSpec(memory_space=pltpu.VMEM),
        scratch_shapes=[
            pltpu.VMEM(boxes.shape, jnp.int32),
            pltpu.VMEM(angle.shape, f32),
            pltpu.VMEM((NX * NC, 8, cols // 2), f32),
            pltpu.VMEM((NX * NC, 8, cols // 2), f32),
            pltpu.VMEM((rows * NZ, PAR * NZ), bf16),
            pltpu.VMEM((NX * NC, NZ, PAR, cols), bf16),
            pltpu.VMEM((rows * NZ, depth), bf16),
            pltpu.VMEM((Q, NX, NC, NY, cols // NY, wide), bf16),
            pltpu.VMEM((Q, R, NZ, part, wide), f32),
            pltpu.VMEM((Q, R, NZ, part, wide), bf16),
            pltpu.VMEM((Q, R, 2, part, wide), bf16),
            pltpu.VMEM((Q, R, 2, part, wide), bf16),
            pltpu.VMEM((Q, R, 2, part, wide // 2), bf16),
            pltpu.VMEM((Q, R, 2, part, wide), bf16),
            pltpu.VMEM((Q, R, 2, part, wide), bf16),
            pltpu.VMEM((WIN * 8, b.shape[1]), bf16),
            dma, dma, dma, dma((Q,)),
            dma((NX * NC,)), dma((NX * NC,)),
            dma((Q, NX)), dma((Q, NX)),
            dma((Q, NX, NY)), dma((Q, NX, NY)),
            dma((Q, NX)), dma((Q, NX)),
            dma((Q, R, 8)), dma((Q, R, 8)),
            dma((Q, 2)), dma((Q, 2)),
        ],
        compiler_params=pltpu.CompilerParams(
            collective_id=0, has_side_effects=True, vmem_limit_bytes=40 * 1024 * 1024),
    )(*[pltpu.with_memory_space_constraint(v, pltpu.HBM) for v in (angle, a, b, boxes)])


def on_device(wedge_local, wedge_ops, octant_angle, child_box):
    a = wedge_local.reshape(NX, NZ, NC, PAR, wedge_local.shape[-1])
    return exchange(octant_angle, a, wedge_ops, child_box.reshape(1, -1))


def solution(mesh):
    placed = (P("box", "dir", None), P(("dir", "box"), None), P(), P(("box", "dir")))
    return jax.shard_map(
        on_device, mesh=mesh, in_specs=placed, out_specs=P(("box", "dir"), None), check_vma=False
    )
```

```python
import jax
import jax.numpy as jnp
from jax import lax
from jax.experimental import pallas as pl
from jax.experimental.pallas import tpu as pltpu
from jax.sharding import PartitionSpec as P

MESH = pl.DeviceIdType.MESH
NX, NZ, NC, NY = 4, 8, 2, 4
PAR = 16
HALO = 4
WIN = PAR + 2 * HALO
Q = 2
R = 2


def kernel(ang_hbm, a_ref, b_ref, box_hbm, out_ref, box_ref, ang_ref, cs_ref, sn_ref, e_ref, abuf, op, bbuf, acc, cpart, relay, near, far, mid,
           relayed, win, lc_sem, lg_sem, la_sem, lb_sem, as_sem, ar_sem, xs_sem, xr_sem, ys_sem, yr_sem, fs_sem, fr_sem,
           cs_sem, cr_sem, hs_sem, hr_sem):
    d = lax.axis_index("dir")
    y = lax.axis_index("box")
    c = d % NC
    z = (d // NC) % NZ
    x = d // (NC * NZ)
    cols = op.shape[1] // (NX * NC)
    wide = bbuf.shape[-1]
    half = cols // 2
    edge = HALO * 8
    part = PAR * 8 // R

    def dev(dx=0, dy=0, dz=0, dc=0):
        return ((((x + dx) % NX) * NZ + (z + dz) % NZ) * NC + (c + dc) % NC, (y + dy) % NY)

    lower = ((d + NX * NZ * NC - 1) % (NX * NZ * NC), y)
    upper = ((d + 1) % (NX * NZ * NC), y)
    corner = ((d + NX * NZ * NC - 1 + 2 * c) % (NX * NZ * NC), y)
    sibling = dev(dc=1)

    barrier = pltpu.get_barrier_semaphore()
    peers = [dev(dx=i, dc=j) for i in range(NX) for j in range(NC) if i or j]
    peers += [dev(dy=i) for i in range(1, NY)]
    peers += [dev(dz=i) for i in (1, 2, NZ - 2, NZ - 1)]
    peers += [corner]
    for p in peers:
        pl.semaphore_signal(barrier, inc=1, device_id=p, device_id_type=MESH)

    def remote(src, dst, send, recv, to):
        return pltpu.make_async_remote_copy(
            src_ref=src, dst_ref=dst, send_sem=send, recv_sem=recv, device_id=to, device_id_type=MESH)

    sent = []

    def push(*args):
        copy = remote(*args)
        copy.start()
        sent.append(copy)

    def arrived(ref, sem):
        remote(ref, ref, sem, sem, sibling).wait_recv()

    angles = pltpu.make_async_copy(ang_hbm, ang_ref, lg_sem)
    angles.start()
    boxes = pltpu.make_async_copy(box_hbm, box_ref, lc_sem)
    boxes.start()
    me = x * NC + c
    own_a = pltpu.make_async_copy(a_ref.at[x, :, c], abuf.at[me], la_sem)
    own_a.start()
    own_b = [pltpu.make_async_copy(b_ref.at[:, pl.ds(q * wide, wide)], bbuf.at[q, x, c, y], lb_sem.at[q])
             for q in range(Q)]
    for copy in own_b:
        copy.start()

    pl.semaphore_wait(barrier, len(peers))

    def send_own(q):
        block = b_ref.at[:, pl.ds(q * wide, wide)]
        for i in (2, 1, 3):
            push(block, bbuf.at[q, x, c, y], xs_sem.at[q, i], xr_sem.at[q, i], dev(dx=i))
        for i in (2, 1, 3):
            push(block, bbuf.at[q, x, c, y], ys_sem.at[q, 0, i], yr_sem.at[q, 0, i], dev(dy=i))

    for q in range(Q):
        send_own(q)
    for i in (2, 1, 3, 0):
        for j in range(NC):
            if i or j:
                push(a_ref.at[(x + i) % NX, :, (c + j) % NC], abuf.at[me],
                     as_sem.at[i * NC + j], ar_sem.at[i * NC + j], dev(dx=i, dc=j))

    row = lax.broadcasted_iota(jnp.int32, e_ref.shape, 0)
    place = (row // 8) % (PAR // R)
    place = jnp.where(row < NZ * part, jnp.where(place < HALO, place, place + PAR - 2 * HALO), place + HALO)
    e_ref[...] = ((row // part) % NZ * PAR + place
                  == lax.broadcasted_iota(jnp.int32, e_ref.shape, 1)).astype(e_ref.dtype)
    angles.wait()
    for i in range(NX):
        for j in range(NC):
            angle = ang_ref[:, pl.ds(i * NZ * NC + z * NC + j, 1), :].reshape(8, half)
            cs_ref[i * NC + j] = jnp.cos(angle)
            sn_ref[i * NC + j] = jnp.sin(angle)

    boxes.wait()
    first = ((y * (NX * NZ * NC) + d) * PAR - HALO) * 8
    place = box_ref[...] - first
    place = jnp.where(place < 2 * edge, place, jnp.where(
        place < 4 * edge, place + edge, jnp.where(place < 5 * edge, place - 2 * edge, place)))
    place = jnp.where(box_ref[...] >= 0, place, -1)
    pick = (lax.broadcasted_iota(jnp.int32, (WIN * 8, place.shape[1]), 0) == place).astype(win.dtype)

    def spread(q):
        for i in (1, 3, 2):
            slot = bbuf.at[q, (x + NX - i) % NX, c, y]
            arrived(slot, xr_sem.at[q, i])
            for k in (1, 3, 2):
                push(slot, slot, ys_sem.at[q, i, k], yr_sem.at[q, i, k], dev(dy=k))

    def collect(q, i):
        if i == 0:
            own_b[q].wait()
        for k in (1, 3, 2):
            arrived(bbuf.at[q, (x + NX - i) % NX, c, (y + NY - k) % NY], yr_sem.at[q, i, k])
        group = bbuf.at[q, (x + NX - i) % NX, c]
        push(group, group, fs_sem.at[q, i], fr_sem.at[q, i], sibling)

    def complete(q):
        for i in range(NX):
            arrived(bbuf.at[q, (x + NX - i) % NX, (c + 1) % NC], fr_sem.at[q, i])

    def turn(k, r):
        rows = NZ * part
        wedge = abuf[k].reshape(NZ * PAR, cols)
        chosen = e_ref[pl.ds(r * rows, rows), :]
        values = jnp.dot(chosen, wedge, preferred_element_type=jnp.float32).reshape(rows // 8, 8, cols)
        re, im = values[..., :half], values[..., half:]
        cosine, sine = cs_ref[k][None], sn_ref[k][None]
        column = pl.multiple_of(k * cols, cols)
        lines = pl.ds(r * rows, rows)
        op[lines, pl.ds(column, half)] = (re * cosine - im * sine).astype(op.dtype).reshape(rows, half)
        op[lines, pl.ds(column + half, half)] = (re * sine + im * cosine).astype(op.dtype).reshape(rows, half)

    for q in range(Q):
        spread(q)
    for q in range(Q):
        collect(q, 0)
    collect(0, 1)
    own_a.wait()
    turn(me, 0)
    for i in (0, 1, 3, 2):
        for j in range(NC):
            if i or j:
                k = ((x + NX - i) % NX) * NC + (c + j) % NC
                arrived(abuf.at[k], ar_sem.at[i * NC + j])
                turn(k, 0)

    low = part // 2

    def multiply(q, r):
        lines = op[pl.ds(r * NZ * part, NZ * part), :]
        weights = bbuf[q].reshape(op.shape[1], wide)
        sums = jnp.dot(lines, weights, preferred_element_type=jnp.float32)
        acc[q, r] = sums.reshape(NZ, part, wide)
        cpart[q, r] = sums.astype(cpart.dtype).reshape(NZ, part, wide)
        for s, sign in enumerate((1, -1)):
            push(cpart.at[q, r, (z + NZ + 3 * sign) % NZ], mid.at[q, r, s],
                 cs_sem.at[q, r, 2 + s], cr_sem.at[q, r, 2 + s], dev(dz=NZ + sign))
        for s, sign in enumerate((1, -1)):
            push(cpart.at[q, r, (z + NZ // 2) % NZ, pl.ds(s * low, low)], far.at[q, r, s],
                 cs_sem.at[q, r, 4 + s], cr_sem.at[q, r, 4 + s], dev(dz=NZ + 2 * sign))

    def adjacent(q, r):
        for s, sign in enumerate((1, -1)):
            push(cpart.at[q, r, (z + NZ + sign) % NZ], near.at[q, r, s],
                 cs_sem.at[q, r, s], cr_sem.at[q, r, s], dev(dz=NZ + sign))

    def forward(q, r):
        for s, sign in enumerate((1, -1)):
            arrived(mid.at[q, r, s], cr_sem.at[q, r, 2 + s])
            arrived(far.at[q, r, s], cr_sem.at[q, r, 4 + s])
            value = acc[q, r, (z + NZ + 2 * sign) % NZ] + mid[q, r, s].astype(jnp.float32)
            extra = far[q, r, s].astype(jnp.float32)
            here, other = pl.ds(s * low, low), pl.ds((1 - s) * low, low)
            relay[q, r, s, here] = (value[s * low:(s + 1) * low] + extra).astype(relay.dtype)
            relay[q, r, s, other] = value[(1 - s) * low:(2 - s) * low].astype(relay.dtype)
            push(relay.at[q, r, s], relayed.at[q, r, s],
                 cs_sem.at[q, r, 6 + s], cr_sem.at[q, r, 6 + s], dev(dz=NZ + 2 * sign))

    def total(q, r):
        value = acc[q, r, z]
        for s in range(2):
            arrived(near.at[q, r, s], cr_sem.at[q, r, s])
            value = value + near[q, r, s].astype(jnp.float32)
        for s in range(2):
            arrived(relayed.at[q, r, s], cr_sem.at[q, r, 6 + s])
            value = value + relayed[q, r, s].astype(jnp.float32)
        here = pl.ds(q * wide, wide)
        win[pl.ds(edge + r * part, part), here] = value.astype(win.dtype)
        if r == 0:
            push(win.at[pl.ds(edge, edge), here], win.at[pl.ds(5 * edge, edge), here],
                 hs_sem.at[q, 0], hr_sem.at[q, 0], lower)
            push(win.at[pl.ds(2 * edge, edge), here], win.at[pl.ds(0, edge), here],
                 hs_sem.at[q, 1], hr_sem.at[q, 1], upper)

    collect(0, 3)
    collect(0, 2)
    complete(0)
    multiply(0, 0)
    for k in range(NX * NC):
        turn(k, 1)
    multiply(0, 1)
    adjacent(0, 0)
    for i in (1, 3, 2):
        collect(1, i)
    complete(1)
    multiply(1, 0)
    adjacent(0, 1)
    multiply(1, 1)
    order = [(q, r) for r in range(R) for q in range(Q)]
    for q, r in order:
        if q:
            adjacent(q, r)
    for q, r in order:
        forward(q, r)
    for q, r in order:
        total(q, r)
    for q in range(Q):
        here = pl.ds(q * wide, wide)
        arrived(win.at[pl.ds(5 * edge, edge), here], hr_sem.at[q, 0])
        arrived(win.at[pl.ds(0, edge), here], hr_sem.at[q, 1])
    out_ref[...] = lax.dot_general(
        pick, win[...], (((0,), (0,)), ((), ())), preferred_element_type=jnp.float32).astype(out_ref.dtype)
    for copy in sent:
        copy.wait_send()


def exchange(angle, a, b, boxes):
    cols, wide = a.shape[-1], b.shape[1] // Q
    rows = PAR * 8
    part = rows // R
    depth = NX * NC * cols
    dma = pltpu.SemaphoreType.DMA
    bf16, f32 = jnp.bfloat16, jnp.float32
    return pl.pallas_call(
        kernel,
        out_shape=jax.ShapeDtypeStruct((boxes.shape[1], b.shape[1]), bf16),
        in_specs=[pl.BlockSpec(memory_space=pltpu.HBM)] * 4,
        out_specs=pl.BlockSpec(memory_space=pltpu.VMEM),
        scratch_shapes=[
            pltpu.VMEM(boxes.shape, jnp.int32),
            pltpu.VMEM(angle.shape, f32),
            pltpu.VMEM((NX * NC, 8, cols // 2), f32),
            pltpu.VMEM((NX * NC, 8, cols // 2), f32),
            pltpu.VMEM((rows * NZ, PAR * NZ), bf16),
            pltpu.VMEM((NX * NC, NZ, PAR, cols), bf16),
            pltpu.VMEM((rows * NZ, depth), bf16),
            pltpu.VMEM((Q, NX, NC, NY, cols // NY, wide), bf16),
            pltpu.VMEM((Q, R, NZ, part, wide), f32),
            pltpu.VMEM((Q, R, NZ, part, wide), bf16),
            pltpu.VMEM((Q, R, 2, part, wide), bf16),
            pltpu.VMEM((Q, R, 2, part, wide), bf16),
            pltpu.VMEM((Q, R, 2, part // 2, wide), bf16),
            pltpu.VMEM((Q, R, 2, part, wide), bf16),
            pltpu.VMEM((Q, R, 2, part, wide), bf16),
            pltpu.VMEM((WIN * 8, b.shape[1]), bf16),
            dma, dma, dma, dma((Q,)),
            dma((NX * NC,)), dma((NX * NC,)),
            dma((Q, NX)), dma((Q, NX)),
            dma((Q, NX, NY)), dma((Q, NX, NY)),
            dma((Q, NX)), dma((Q, NX)),
            dma((Q, R, 8)), dma((Q, R, 8)),
            dma((Q, 2)), dma((Q, 2)),
        ],
        compiler_params=pltpu.CompilerParams(
            collective_id=0, has_side_effects=True, vmem_limit_bytes=40 * 1024 * 1024),
    )(*[pltpu.with_memory_space_constraint(v, pltpu.HBM) for v in (angle, a, b, boxes)])


def on_device(wedge_local, wedge_ops, octant_angle, child_box):
    a = wedge_local.reshape(NX, NZ, NC, PAR, wedge_local.shape[-1])
    return exchange(octant_angle, a, wedge_ops, child_box.reshape(1, -1))


def solution(mesh):
    placed = (P("box", "dir", None), P(("dir", "box"), None), P(), P(("box", "dir")))
    return jax.shard_map(
        on_device, mesh=mesh, in_specs=placed, out_specs=P(("box", "dir"), None), check_vma=False
    )
```

```python
import jax
import jax.numpy as jnp
from jax import lax
from jax.experimental import pallas as pl
from jax.experimental.pallas import tpu as pltpu
from jax.sharding import PartitionSpec as P

MESH = pl.DeviceIdType.MESH
NX, NZ, NC, NY = 4, 8, 2, 4
PAR = 16
HALO = 4
WIN = PAR + 2 * HALO
Q = 2
R = 2


def kernel(ang_hbm, a_ref, b_ref, box_hbm, out_ref, box_ref, ang_ref, cs_ref, sn_ref, e_ref, abuf, op, bbuf, acc, cpart, relay, near, far, mid,
           relayed, win, lc_sem, lg_sem, la_sem, lb_sem, as_sem, ar_sem, xs_sem, xr_sem, ys_sem, yr_sem, fs_sem, fr_sem,
           cs_sem, cr_sem, hs_sem, hr_sem):
    d = lax.axis_index("dir")
    y = lax.axis_index("box")
    c = d % NC
    z = (d // NC) % NZ
    x = d // (NC * NZ)
    cols = op.shape[1] // (NX * NC)
    wide = bbuf.shape[-1]
    half = cols // 2
    edge = HALO * 8
    part = PAR * 8 // R

    def dev(dx=0, dy=0, dz=0, dc=0):
        return ((((x + dx) % NX) * NZ + (z + dz) % NZ) * NC + (c + dc) % NC, (y + dy) % NY)

    lower = ((d + NX * NZ * NC - 1) % (NX * NZ * NC), y)
    upper = ((d + 1) % (NX * NZ * NC), y)
    corner = ((d + NX * NZ * NC - 1 + 2 * c) % (NX * NZ * NC), y)
    sibling = dev(dc=1)

    barrier = pltpu.get_barrier_semaphore()
    peers = [dev(dx=i, dc=j) for i in range(NX) for j in range(NC) if i or j]
    peers += [dev(dy=i) for i in range(1, NY)]
    peers += [dev(dz=i) for i in (1, 2, NZ - 2, NZ - 1)]
    peers += [corner]
    for p in peers:
        pl.semaphore_signal(barrier, inc=1, device_id=p, device_id_type=MESH)

    def remote(src, dst, send, recv, to):
        return pltpu.make_async_remote_copy(
            src_ref=src, dst_ref=dst, send_sem=send, recv_sem=recv, device_id=to, device_id_type=MESH)

    sent = []

    def push(*args):
        copy = remote(*args)
        copy.start()
        sent.append(copy)

    def arrived(ref, sem):
        remote(ref, ref, sem, sem, sibling).wait_recv()

    angles = pltpu.make_async_copy(ang_hbm, ang_ref, lg_sem)
    angles.start()
    boxes = pltpu.make_async_copy(box_hbm, box_ref, lc_sem)
    boxes.start()
    me = x * NC + c
    own_a = pltpu.make_async_copy(a_ref.at[x, :, c], abuf.at[me], la_sem)
    own_a.start()
    own_b = [pltpu.make_async_copy(b_ref.at[:, pl.ds(q * wide, wide)], bbuf.at[q, x, c, y], lb_sem.at[q])
             for q in range(Q)]
    for copy in own_b:
        copy.start()

    pl.semaphore_wait(barrier, len(peers))

    def send_own(q):
        block = b_ref.at[:, pl.ds(q * wide, wide)]
        for i in (2, 1, 3):
            push(block, bbuf.at[q, x, c, y], xs_sem.at[q, i], xr_sem.at[q, i], dev(dx=i))
        for i in (2, 1, 3):
            push(block, bbuf.at[q, x, c, y], ys_sem.at[q, 0, i], yr_sem.at[q, 0, i], dev(dy=i))

    for q in range(Q):
        send_own(q)
    for i in (2, 1, 3, 0):
        for j in range(NC):
            if i or j:
                push(a_ref.at[(x + i) % NX, :, (c + j) % NC], abuf.at[me],
                     as_sem.at[i * NC + j], ar_sem.at[i * NC + j], dev(dx=i, dc=j))

    row = lax.broadcasted_iota(jnp.int32, e_ref.shape, 0)
    place = (row // 8) % (PAR // R)
    place = jnp.where(row < NZ * part, jnp.where(place < HALO, place, place + PAR - 2 * HALO), place + HALO)
    e_ref[...] = ((row // part) % NZ * PAR + place
                  == lax.broadcasted_iota(jnp.int32, e_ref.shape, 1)).astype(e_ref.dtype)
    angles.wait()
    for i in range(NX):
        for j in range(NC):
            angle = ang_ref[:, pl.ds(i * NZ * NC + z * NC + j, 1), :].reshape(8, half)
            cs_ref[i * NC + j] = jnp.cos(angle)
            sn_ref[i * NC + j] = jnp.sin(angle)

    boxes.wait()
    first = ((y * (NX * NZ * NC) + d) * PAR - HALO) * 8
    place = box_ref[...] - first
    place = jnp.where(place < 2 * edge, place, jnp.where(
        place < 4 * edge, place + edge, jnp.where(place < 5 * edge, place - 2 * edge, place)))
    place = jnp.where(box_ref[...] >= 0, place, -1)
    pick = (lax.broadcasted_iota(jnp.int32, (WIN * 8, place.shape[1]), 0) == place).astype(win.dtype)

    def spread(q):
        for i in (1, 3, 2):
            slot = bbuf.at[q, (x + NX - i) % NX, c, y]
            arrived(slot, xr_sem.at[q, i])
            for k in (1, 3, 2):
                push(slot, slot, ys_sem.at[q, i, k], yr_sem.at[q, i, k], dev(dy=k))

    def collect(q, i):
        if i == 0:
            own_b[q].wait()
        for k in (1, 3, 2):
            arrived(bbuf.at[q, (x + NX - i) % NX, c, (y + NY - k) % NY], yr_sem.at[q, i, k])
        group = bbuf.at[q, (x + NX - i) % NX, c]
        push(group, group, fs_sem.at[q, i], fr_sem.at[q, i], sibling)

    def complete(q):
        for i in range(NX):
            arrived(bbuf.at[q, (x + NX - i) % NX, (c + 1) % NC], fr_sem.at[q, i])

    def turn(k, r):
        rows = NZ * part
        wedge = abuf[k].reshape(NZ * PAR, cols)
        chosen = e_ref[pl.ds(r * rows, rows), :]
        values = jnp.dot(chosen, wedge, preferred_element_type=jnp.float32).reshape(rows // 8, 8, cols)
        re, im = values[..., :half], values[..., half:]
        cosine, sine = cs_ref[k][None], sn_ref[k][None]
        column = pl.multiple_of(k * cols, cols)
        lines = pl.ds(r * rows, rows)
        op[lines, pl.ds(column, half)] = (re * cosine - im * sine).astype(op.dtype).reshape(rows, half)
        op[lines, pl.ds(column + half, half)] = (re * sine + im * cosine).astype(op.dtype).reshape(rows, half)

    for q in range(Q):
        spread(q)
    for q in range(Q):
        collect(q, 0)
    collect(0, 1)
    own_a.wait()
    turn(me, 0)
    for i in (0, 1, 3, 2):
        for j in range(NC):
            if i or j:
                k = ((x + NX - i) % NX) * NC + (c + j) % NC
                arrived(abuf.at[k], ar_sem.at[i * NC + j])
                turn(k, 0)

    low = part // 2

    def multiply(q, r):
        lines = op[pl.ds(r * NZ * part, NZ * part), :]
        weights = bbuf[q].reshape(op.shape[1], wide)
        sums = jnp.dot(lines, weights, preferred_element_type=jnp.float32)
        acc[q, r] = sums.reshape(NZ, part, wide)
        cpart[q, r] = sums.astype(cpart.dtype).reshape(NZ, part, wide)
        for s, sign in enumerate((1, -1)):
            push(cpart.at[q, r, (z + NZ + 3 * sign) % NZ], mid.at[q, r, s],
                 cs_sem.at[q, r, 2 + s], cr_sem.at[q, r, 2 + s], dev(dz=NZ + sign))
        for s, sign in enumerate((1, -1)):
            push(cpart.at[q, r, (z + NZ // 2) % NZ, pl.ds(s * low, low)], far.at[q, r, s],
                 cs_sem.at[q, r, 4 + s], cr_sem.at[q, r, 4 + s], dev(dz=NZ + 2 * sign))

    def adjacent(q, r):
        for s, sign in enumerate((1, -1)):
            push(cpart.at[q, r, (z + NZ + sign) % NZ], near.at[q, r, s],
                 cs_sem.at[q, r, s], cr_sem.at[q, r, s], dev(dz=NZ + sign))

    def forward(q, r):
        for s, sign in enumerate((1, -1)):
            arrived(mid.at[q, r, s], cr_sem.at[q, r, 2 + s])
            arrived(far.at[q, r, s], cr_sem.at[q, r, 4 + s])
            value = acc[q, r, (z + NZ + 2 * sign) % NZ] + mid[q, r, s].astype(jnp.float32)
            extra = far[q, r, s].astype(jnp.float32)
            here, other = pl.ds(s * low, low), pl.ds((1 - s) * low, low)
            relay[q, r, s, here] = (value[s * low:(s + 1) * low] + extra).astype(relay.dtype)
            relay[q, r, s, other] = value[(1 - s) * low:(2 - s) * low].astype(relay.dtype)
            push(relay.at[q, r, s], relayed.at[q, r, s],
                 cs_sem.at[q, r, 6 + s], cr_sem.at[q, r, 6 + s], dev(dz=NZ + 2 * sign))

    def total(q, r):
        value = acc[q, r, z]
        for s in range(2):
            arrived(near.at[q, r, s], cr_sem.at[q, r, s])
            value = value + near[q, r, s].astype(jnp.float32)
        for s in range(2):
            arrived(relayed.at[q, r, s], cr_sem.at[q, r, 6 + s])
            value = value + relayed[q, r, s].astype(jnp.float32)
        here = pl.ds(q * wide, wide)
        win[pl.ds(edge + r * part, part), here] = value.astype(win.dtype)
        if r == 0:
            push(win.at[pl.ds(edge, edge), here], win.at[pl.ds(5 * edge, edge), here],
                 hs_sem.at[q, 0], hr_sem.at[q, 0], lower)
            push(win.at[pl.ds(2 * edge, edge), here], win.at[pl.ds(0, edge), here],
                 hs_sem.at[q, 1], hr_sem.at[q, 1], upper)

    collect(0, 3)
    collect(0, 2)
    complete(0)
    multiply(0, 0)
    for k in range(NX * NC):
        turn(k, 1)
    multiply(0, 1)
    adjacent(0, 0)
    adjacent(0, 1)
    for i in (1, 3, 2):
        collect(1, i)
    complete(1)
    multiply(1, 0)
    adjacent(1, 0)
    multiply(1, 1)
    adjacent(1, 1)
    order = [(q, r) for r in range(R) for q in range(Q)]
    for q, r in order:
        forward(q, r)
    for q, r in order:
        total(q, r)
    for q in range(Q):
        here = pl.ds(q * wide, wide)
        arrived(win.at[pl.ds(5 * edge, edge), here], hr_sem.at[q, 0])
        arrived(win.at[pl.ds(0, edge), here], hr_sem.at[q, 1])
    out_ref[...] = lax.dot_general(
        pick, win[...], (((0,), (0,)), ((), ())), preferred_element_type=jnp.float32).astype(out_ref.dtype)
    for copy in sent:
        copy.wait_send()


def exchange(angle, a, b, boxes):
    cols, wide = a.shape[-1], b.shape[1] // Q
    rows = PAR * 8
    part = rows // R
    depth = NX * NC * cols
    dma = pltpu.SemaphoreType.DMA
    bf16, f32 = jnp.bfloat16, jnp.float32
    return pl.pallas_call(
        kernel,
        out_shape=jax.ShapeDtypeStruct((boxes.shape[1], b.shape[1]), bf16),
        in_specs=[pl.BlockSpec(memory_space=pltpu.HBM)] * 4,
        out_specs=pl.BlockSpec(memory_space=pltpu.VMEM),
        scratch_shapes=[
            pltpu.VMEM(boxes.shape, jnp.int32),
            pltpu.VMEM(angle.shape, f32),
            pltpu.VMEM((NX * NC, 8, cols // 2), f32),
            pltpu.VMEM((NX * NC, 8, cols // 2), f32),
            pltpu.VMEM((rows * NZ, PAR * NZ), bf16),
            pltpu.VMEM((NX * NC, NZ, PAR, cols), bf16),
            pltpu.VMEM((rows * NZ, depth), bf16),
            pltpu.VMEM((Q, NX, NC, NY, cols // NY, wide), bf16),
            pltpu.VMEM((Q, R, NZ, part, wide), f32),
            pltpu.VMEM((Q, R, NZ, part, wide), bf16),
            pltpu.VMEM((Q, R, 2, part, wide), bf16),
            pltpu.VMEM((Q, R, 2, part, wide), bf16),
            pltpu.VMEM((Q, R, 2, part // 2, wide), bf16),
            pltpu.VMEM((Q, R, 2, part, wide), bf16),
            pltpu.VMEM((Q, R, 2, part, wide), bf16),
            pltpu.VMEM((WIN * 8, b.shape[1]), bf16),
            dma, dma, dma, dma((Q,)),
            dma((NX * NC,)), dma((NX * NC,)),
            dma((Q, NX)), dma((Q, NX)),
            dma((Q, NX, NY)), dma((Q, NX, NY)),
            dma((Q, NX)), dma((Q, NX)),
            dma((Q, R, 8)), dma((Q, R, 8)),
            dma((Q, 2)), dma((Q, 2)),
        ],
        compiler_params=pltpu.CompilerParams(
            collective_id=0, has_side_effects=True, vmem_limit_bytes=40 * 1024 * 1024),
    )(*[pltpu.with_memory_space_constraint(v, pltpu.HBM) for v in (angle, a, b, boxes)])


def on_device(wedge_local, wedge_ops, octant_angle, child_box):
    a = wedge_local.reshape(NX, NZ, NC, PAR, wedge_local.shape[-1])
    return exchange(octant_angle, a, wedge_ops, child_box.reshape(1, -1))


def solution(mesh):
    placed = (P("box", "dir", None), P(("dir", "box"), None), P(), P(("box", "dir")))
    return jax.shard_map(
        on_device, mesh=mesh, in_specs=placed, out_specs=P(("box", "dir"), None), check_vma=False
    )
```

```python
import jax
import jax.numpy as jnp
from jax import lax
from jax.experimental import pallas as pl
from jax.experimental.pallas import tpu as pltpu
from jax.sharding import PartitionSpec as P

MESH = pl.DeviceIdType.MESH
NX, NZ, NC, NY = 4, 8, 2, 4
PAR = 16
HALO = 4
WIN = PAR + 2 * HALO
Q = 2
R = 2


def kernel(ang_hbm, a_ref, b_ref, box_hbm, out_ref, box_ref, ang_ref, cs_ref, sn_ref, e_ref, abuf, op, bbuf, acc, cpart, relay, near, far, mid,
           relayed, win, lc_sem, lg_sem, la_sem, lb_sem, as_sem, ar_sem, xs_sem, xr_sem, ys_sem, yr_sem, fs_sem, fr_sem,
           cs_sem, cr_sem, hs_sem, hr_sem):
    d = lax.axis_index("dir")
    y = lax.axis_index("box")
    c = d % NC
    z = (d // NC) % NZ
    x = d // (NC * NZ)
    cols = op.shape[1] // (NX * NC)
    wide = bbuf.shape[-1]
    half = cols // 2
    edge = HALO * 8
    part = PAR * 8 // R

    def dev(dx=0, dy=0, dz=0, dc=0):
        return ((((x + dx) % NX) * NZ + (z + dz) % NZ) * NC + (c + dc) % NC, (y + dy) % NY)

    lower = ((d + NX * NZ * NC - 1) % (NX * NZ * NC), y)
    upper = ((d + 1) % (NX * NZ * NC), y)
    corner = ((d + NX * NZ * NC - 1 + 2 * c) % (NX * NZ * NC), y)
    sibling = dev(dc=1)

    barrier = pltpu.get_barrier_semaphore()
    peers = [dev(dx=i, dc=j) for i in range(NX) for j in range(NC) if i or j]
    peers += [dev(dy=i) for i in range(1, NY)]
    peers += [dev(dz=i) for i in (1, 2, NZ - 2, NZ - 1)]
    peers += [corner]
    for p in peers:
        pl.semaphore_signal(barrier, inc=1, device_id=p, device_id_type=MESH)

    def remote(src, dst, send, recv, to):
        return pltpu.make_async_remote_copy(
            src_ref=src, dst_ref=dst, send_sem=send, recv_sem=recv, device_id=to, device_id_type=MESH)

    sent = []

    def push(*args):
        copy = remote(*args)
        copy.start()
        sent.append(copy)

    def arrived(ref, sem):
        remote(ref, ref, sem, sem, sibling).wait_recv()

    angles = pltpu.make_async_copy(ang_hbm, ang_ref, lg_sem)
    angles.start()
    boxes = pltpu.make_async_copy(box_hbm, box_ref, lc_sem)
    boxes.start()
    me = x * NC + c
    own_a = pltpu.make_async_copy(a_ref.at[x, :, c], abuf.at[me], la_sem)
    own_a.start()
    own_b = [pltpu.make_async_copy(b_ref.at[:, pl.ds(q * wide, wide)], bbuf.at[q, x, c, y], lb_sem.at[q])
             for q in range(Q)]
    for copy in own_b:
        copy.start()

    pl.semaphore_wait(barrier, len(peers))

    blocks = [b_ref.at[:, pl.ds(q * wide, wide)] for q in range(Q)]
    for q in range(Q):
        for i in (2, 1, 3):
            push(blocks[q], bbuf.at[q, x, c, y], xs_sem.at[q, i], xr_sem.at[q, i], dev(dx=i))
    for q in range(Q):
        for i in (2, 1, 3):
            push(blocks[q], bbuf.at[q, x, c, y], ys_sem.at[q, 0, i], yr_sem.at[q, 0, i], dev(dy=i))
    for i in (2, 1, 3, 0):
        for j in range(NC):
            if i or j:
                push(a_ref.at[(x + i) % NX, :, (c + j) % NC], abuf.at[me],
                     as_sem.at[i * NC + j], ar_sem.at[i * NC + j], dev(dx=i, dc=j))

    row = lax.broadcasted_iota(jnp.int32, e_ref.shape, 0)
    place = (row // 8) % (PAR // R)
    place = jnp.where(row < NZ * part, jnp.where(place < HALO, place, place + PAR - 2 * HALO), place + HALO)
    e_ref[...] = ((row // part) % NZ * PAR + place
                  == lax.broadcasted_iota(jnp.int32, e_ref.shape, 1)).astype(e_ref.dtype)
    angles.wait()
    for i in range(NX):
        for j in range(NC):
            angle = ang_ref[:, pl.ds(i * NZ * NC + z * NC + j, 1), :].reshape(8, half)
            cs_ref[i * NC + j] = jnp.cos(angle)
            sn_ref[i * NC + j] = jnp.sin(angle)

    boxes.wait()
    first = ((y * (NX * NZ * NC) + d) * PAR - HALO) * 8
    place = box_ref[...] - first
    place = jnp.where(place < 2 * edge, place, jnp.where(
        place < 4 * edge, place + edge, jnp.where(place < 5 * edge, place - 2 * edge, place)))
    place = jnp.where(box_ref[...] >= 0, place, -1)
    pick = (lax.broadcasted_iota(jnp.int32, (WIN * 8, place.shape[1]), 0) == place).astype(win.dtype)

    def spread(q):
        for i in (1, 3, 2):
            slot = bbuf.at[q, (x + NX - i) % NX, c, y]
            arrived(slot, xr_sem.at[q, i])
            for k in (1, 3, 2):
                push(slot, slot, ys_sem.at[q, i, k], yr_sem.at[q, i, k], dev(dy=k))

    def collect(q, i):
        if i == 0:
            own_b[q].wait()
        for k in (1, 3, 2):
            arrived(bbuf.at[q, (x + NX - i) % NX, c, (y + NY - k) % NY], yr_sem.at[q, i, k])
        group = bbuf.at[q, (x + NX - i) % NX, c]
        push(group, group, fs_sem.at[q, i], fr_sem.at[q, i], sibling)

    def complete(q):
        for i in range(NX):
            arrived(bbuf.at[q, (x + NX - i) % NX, (c + 1) % NC], fr_sem.at[q, i])

    def turn(k, r):
        rows = NZ * part
        wedge = abuf[k].reshape(NZ * PAR, cols)
        chosen = e_ref[pl.ds(r * rows, rows), :]
        values = jnp.dot(chosen, wedge, preferred_element_type=jnp.float32).reshape(rows // 8, 8, cols)
        re, im = values[..., :half], values[..., half:]
        cosine, sine = cs_ref[k][None], sn_ref[k][None]
        column = pl.multiple_of(k * cols, cols)
        lines = pl.ds(r * rows, rows)
        op[lines, pl.ds(column, half)] = (re * cosine - im * sine).astype(op.dtype).reshape(rows, half)
        op[lines, pl.ds(column + half, half)] = (re * sine + im * cosine).astype(op.dtype).reshape(rows, half)

    for q in range(Q):
        spread(q)
    for q in range(Q):
        collect(q, 0)
    collect(0, 1)
    own_a.wait()
    turn(me, 0)
    for i in (0, 1, 3, 2):
        for j in range(NC):
            if i or j:
                k = ((x + NX - i) % NX) * NC + (c + j) % NC
                arrived(abuf.at[k], ar_sem.at[i * NC + j])
                turn(k, 0)

    low = part // 2

    def multiply(q, r):
        lines = op[pl.ds(r * NZ * part, NZ * part), :]
        weights = bbuf[q].reshape(op.shape[1], wide)
        sums = jnp.dot(lines, weights, preferred_element_type=jnp.float32)
        acc[q, r] = sums.reshape(NZ, part, wide)
        cpart[q, r] = sums.astype(cpart.dtype).reshape(NZ, part, wide)
        for s, sign in enumerate((1, -1)):
            push(cpart.at[q, r, (z + NZ + 3 * sign) % NZ], mid.at[q, r, s],
                 cs_sem.at[q, r, 2 + s], cr_sem.at[q, r, 2 + s], dev(dz=NZ + sign))
        for s, sign in enumerate((1, -1)):
            push(cpart.at[q, r, (z + NZ // 2) % NZ, pl.ds(s * low, low)], far.at[q, r, s],
                 cs_sem.at[q, r, 4 + s], cr_sem.at[q, r, 4 + s], dev(dz=NZ + 2 * sign))

    def adjacent(q, r):
        for s, sign in enumerate((1, -1)):
            push(cpart.at[q, r, (z + NZ + sign) % NZ], near.at[q, r, s],
                 cs_sem.at[q, r, s], cr_sem.at[q, r, s], dev(dz=NZ + sign))

    def forward(q, r):
        for s, sign in enumerate((1, -1)):
            arrived(mid.at[q, r, s], cr_sem.at[q, r, 2 + s])
            arrived(far.at[q, r, s], cr_sem.at[q, r, 4 + s])
            value = acc[q, r, (z + NZ + 2 * sign) % NZ] + mid[q, r, s].astype(jnp.float32)
            extra = far[q, r, s].astype(jnp.float32)
            here, other = pl.ds(s * low, low), pl.ds((1 - s) * low, low)
            relay[q, r, s, here] = (value[s * low:(s + 1) * low] + extra).astype(relay.dtype)
            relay[q, r, s, other] = value[(1 - s) * low:(2 - s) * low].astype(relay.dtype)
            push(relay.at[q, r, s], relayed.at[q, r, s],
                 cs_sem.at[q, r, 6 + s], cr_sem.at[q, r, 6 + s], dev(dz=NZ + 2 * sign))

    def total(q, r):
        value = acc[q, r, z]
        for s in range(2):
            arrived(near.at[q, r, s], cr_sem.at[q, r, s])
            value = value + near[q, r, s].astype(jnp.float32)
        for s in range(2):
            arrived(relayed.at[q, r, s], cr_sem.at[q, r, 6 + s])
            value = value + relayed[q, r, s].astype(jnp.float32)
        here = pl.ds(q * wide, wide)
        win[pl.ds(edge + r * part, part), here] = value.astype(win.dtype)
        if r == 0:
            push(win.at[pl.ds(edge, edge), here], win.at[pl.ds(5 * edge, edge), here],
                 hs_sem.at[q, 0], hr_sem.at[q, 0], lower)
            push(win.at[pl.ds(2 * edge, edge), here], win.at[pl.ds(0, edge), here],
                 hs_sem.at[q, 1], hr_sem.at[q, 1], upper)

    collect(0, 3)
    collect(0, 2)
    complete(0)
    multiply(0, 0)
    for k in range(NX * NC):
        turn(k, 1)
    multiply(0, 1)
    adjacent(0, 0)
    adjacent(0, 1)
    for i in (1, 3, 2):
        collect(1, i)
    complete(1)
    multiply(1, 0)
    adjacent(1, 0)
    multiply(1, 1)
    adjacent(1, 1)
    order = [(q, r) for r in range(R) for q in range(Q)]
    for q, r in order:
        forward(q, r)
    for q, r in order:
        total(q, r)
    for q in range(Q):
        here = pl.ds(q * wide, wide)
        arrived(win.at[pl.ds(5 * edge, edge), here], hr_sem.at[q, 0])
        arrived(win.at[pl.ds(0, edge), here], hr_sem.at[q, 1])
    out_ref[...] = lax.dot_general(
        pick, win[...], (((0,), (0,)), ((), ())), preferred_element_type=jnp.float32).astype(out_ref.dtype)
    for copy in sent:
        copy.wait_send()


def exchange(angle, a, b, boxes):
    cols, wide = a.shape[-1], b.shape[1] // Q
    rows = PAR * 8
    part = rows // R
    depth = NX * NC * cols
    dma = pltpu.SemaphoreType.DMA
    bf16, f32 = jnp.bfloat16, jnp.float32
    return pl.pallas_call(
        kernel,
        out_shape=jax.ShapeDtypeStruct((boxes.shape[1], b.shape[1]), bf16),
        in_specs=[pl.BlockSpec(memory_space=pltpu.HBM)] * 4,
        out_specs=pl.BlockSpec(memory_space=pltpu.VMEM),
        scratch_shapes=[
            pltpu.VMEM(boxes.shape, jnp.int32),
            pltpu.VMEM(angle.shape, f32),
            pltpu.VMEM((NX * NC, 8, cols // 2), f32),
            pltpu.VMEM((NX * NC, 8, cols // 2), f32),
            pltpu.VMEM((rows * NZ, PAR * NZ), bf16),
            pltpu.VMEM((NX * NC, NZ, PAR, cols), bf16),
            pltpu.VMEM((rows * NZ, depth), bf16),
            pltpu.VMEM((Q, NX, NC, NY, cols // NY, wide), bf16),
            pltpu.VMEM((Q, R, NZ, part, wide), f32),
            pltpu.VMEM((Q, R, NZ, part, wide), bf16),
            pltpu.VMEM((Q, R, 2, part, wide), bf16),
            pltpu.VMEM((Q, R, 2, part, wide), bf16),
            pltpu.VMEM((Q, R, 2, part // 2, wide), bf16),
            pltpu.VMEM((Q, R, 2, part, wide), bf16),
            pltpu.VMEM((Q, R, 2, part, wide), bf16),
            pltpu.VMEM((WIN * 8, b.shape[1]), bf16),
            dma, dma, dma, dma((Q,)),
            dma((NX * NC,)), dma((NX * NC,)),
            dma((Q, NX)), dma((Q, NX)),
            dma((Q, NX, NY)), dma((Q, NX, NY)),
            dma((Q, NX)), dma((Q, NX)),
            dma((Q, R, 8)), dma((Q, R, 8)),
            dma((Q, 2)), dma((Q, 2)),
        ],
        compiler_params=pltpu.CompilerParams(
            collective_id=0, has_side_effects=True, vmem_limit_bytes=40 * 1024 * 1024),
    )(*[pltpu.with_memory_space_constraint(v, pltpu.HBM) for v in (angle, a, b, boxes)])


def on_device(wedge_local, wedge_ops, octant_angle, child_box):
    a = wedge_local.reshape(NX, NZ, NC, PAR, wedge_local.shape[-1])
    return exchange(octant_angle, a, wedge_ops, child_box.reshape(1, -1))


def solution(mesh):
    placed = (P("box", "dir", None), P(("dir", "box"), None), P(), P(("box", "dir")))
    return jax.shard_map(
        on_device, mesh=mesh, in_specs=placed, out_specs=P(("box", "dir"), None), check_vma=False
    )
```
